32 devices in a mesh: paths: 2 (over x), trades: 8 (over z, y), quad: 2 (over core).
Axes of the slice: x: 2, y: 2, z: 4, core: 2. Of those that a mesh axis runs over, the one named last changes fastest.
Arguments:
- factor_paths: bfloat16 [8192, 4, 256], P(('trades', 'quad'), None, 'paths'), parts along dimension 2, may hold values from -6 to 6
- loadings: bfloat16 [16384, 64], P(('trades', 'quad')), may hold values from -0.75 to 0.75
- coeffs: bfloat16 [16384, 64], P(('trades', 'quad')), may hold values from -0.09375 to 0.09375
- trade_blocks: int32 [16384, 4], P(('trades', 'quad')), may hold values from 0 to 511, all different within a row; in each aligned block of 1024 rows (0 to 1023, 1024 to 2047, ...) at most 16 rows name the same one
- trade_set: int32 [16384], P(('trades', 'quad')), may hold values from 0 to 383
- set_order: int32 [384], replicated, may hold values from 0 to 383, each once
- owner_counts: int32 [16], replicated, may hold values from 1 to 32, 384 in all
Outputs:
- exposure: float32 [512, 4, 256], P(('trades', 'quad'), None, 'paths'), parts along dimension 2
The draws below stay inside these ranges and needn't reach their ends.
There are 2 independent parts, one for each index of `paths`. The reference program is written for one: setup_inputs(seed, part) draws one part's arguments, and reference() takes and returns one part's arrays. A program takes and returns all parts, laid end to end along the dimension named above; an argument that names none is the same for every part. Nothing has to cross between parts.
Inputs may be any that keep to these rules, and one draw needn't show every extreme that they name: `trade_blocks`: the 4 blocks of a trade are different; among the trades of one device (aligned blocks of 1024 rows) no block is named by more than 16 trades, and some block by exactly 16. `set_order`: each rank occurs once. `owner_counts`: they sum to 384; some device owns exactly 32.
All inputs are finite; a program needn't handle non-finite values.
Results may differ from the reference program's by a relative error of at most 0.0023.
Values may be sent and summed in bfloat16 or wider, within the bound.
A program may use at most 128 MiB of HBM per device.

```python
import math
import jax
import jax.numpy as jnp
import numpy as np
from jax import lax

FACTORS = 8192
BLOCK_LEN = 16
REFS = 4
HIT_CAP = 16
BASIS = 64
PATHS = 128
DATES = 4
TRADE_DEV = 1024
SET_CAP = 32
OWNERS = 16
TRADES = 16384
BLOCKS = 512
NSETS = 384


def place_ends(array, key, least, top_value):
    shape = array.shape
    index_at = [jax.random.randint(jax.random.fold_in(key, axis), (), 0, shape[axis]) for axis in range(len(shape))]
    array = array.at[tuple(index_at)].set(least)
    longest = shape.index(max(shape))
    index_at[longest] = (index_at[longest] + 1) % shape[longest]
    return array.at[tuple(index_at)].set(top_value)


def steps_of(rng, extent, cuts, smallest, top_value):
    gain, own = 1.0, jax.random.fold_in(rng, 6)
    for dim, shards_of in cuts:
        draws = jnp.exp(jax.random.uniform(jax.random.fold_in(own, dim), (shards_of,), jnp.float32, smallest / len(cuts), top_value / len(cuts)))
        gain = gain * jnp.repeat(draws, extent[dim] // shards_of).reshape([-1 if axis == dim else 1 for axis in range(len(extent))])
    return gain


def length_profile(number_of, total, reach, skew):
    loads = [(1 << 20) // math.isqrt(grade ** skew) + 1 for grade in range(2, number_of + 1)]
    rest, given = total - reach - (number_of - 1), [1] * (number_of - 1)
    while rest > 0:
        movable = [i for i in range(number_of - 1) if given[i] < reach]
        mass, remaining = sum([loads[i] for i in movable]), rest
        for i in movable:
            extra = min(reach - given[i], max(1, remaining * loads[i] // mass), rest)
            given[i] = given[i] + extra
            rest = rest - extra
    return np.array([reach] + given)


def ragged_sizes(own_key, amount, total, most, lean):
    if amount == 2:
        one = jax.random.randint(own_key, (), max(1, total - most), min(most, total - 1) + 1)
        return jnp.stack([one, total - one])
    lengths = jnp.asarray(length_profile(amount, total, most, lean), jnp.int32)
    pairs = (amount - 1) // 2
    giver, receiver = lengths[1:1 + 2 * pairs:2], lengths[2:2 + 2 * pairs:2]
    margin = jnp.minimum(giver - 1, most - receiver)
    shifted = jax.random.randint(jax.random.fold_in(own_key, 1), (pairs,), 0, 1 << 20) % (margin + 1)
    lengths = lengths.at[1:1 + 2 * pairs:2].set(giver - shifted).at[2:2 + 2 * pairs:2].set(receiver + shifted)
    return lengths[jax.random.permutation(jax.random.fold_in(own_key, 2), amount)]


def shared_out(key, own, number, rows, amount, top, most, lean):
    order = jax.random.permutation(key, amount)
    packed, usual = portions_of(amount, rows * top, most, lean, True), portions_of(amount, rows * top, most, lean, False)
    places = jnp.arange(amount)

    def named(tallies, turn):
        used = int((tallies > 0).sum())
        fixed = max(1, used // 4)
        moved = fixed + (places - fixed + turn * (used - fixed)) % max(1, amount - fixed)
        return jnp.zeros((amount,), jnp.int32).at[order[jnp.where(places < fixed, places, moved)]].set(jnp.asarray(tallies, jnp.int32))

    tallies = jnp.where(number % 4 == 0, named(packed, number // 4), named(usual, number - number // 4 - 1))
    mixed = jax.random.permutation(jax.random.fold_in(own, 3), amount)
    source_of, taker = mixed[0:amount // 2 * 2:2], mixed[1:amount // 2 * 2:2]
    room = jnp.minimum(tallies[source_of] - 1, most - tallies[taker]) // 2
    room = jnp.where((source_of == order[0]) | (taker == order[0]) | (tallies[taker] == 0), 0, jnp.maximum(room, 0))
    moved = jax.random.randint(jax.random.fold_in(own, 4), (amount // 2,), 0, 1 << 20) % (room + 1)
    tallies = tallies.at[source_of].add(-moved).at[taker].add(moved)
    members = jnp.searchsorted(jnp.cumsum(tallies), jnp.arange(rows * top), side="right").astype(jnp.int32)
    grid = members.reshape(top, rows).T
    grid = grid[jax.random.permutation(jax.random.fold_in(own, 1), rows)]
    turn = jax.random.randint(jax.random.fold_in(own, 2), (rows, 1), 0, top)
    return jnp.take_along_axis(grid, (jnp.arange(top)[None, :] + turn) % top, axis=1)


def portions_of(number_of, total, reach, slope, full):
    weights = [(1 << 20) // math.isqrt(grade ** slope) + 1 for grade in range(1, number_of + 1)]
    largest = reach if full else min(reach, max(-(-total // number_of), total * weights[0] // sum(weights)))
    least = 1 if total - largest >= number_of - 1 else 0
    counts, spare = [largest] + [least] * (number_of - 1), total - largest - least * (number_of - 1)
    while spare > 0:
        candidates = [i for i in range(1, number_of) if counts[i] < largest] or [i for i in range(1, number_of) if counts[i] < reach]
        pool, budget = sum([weights[i] for i in candidates]), spare
        for i in candidates:
            extra = min(reach - counts[i], max(1, budget * weights[i] // pool), spare)
            counts[i] = counts[i] + extra
            spare = spare - extra
    return np.array(counts)


def bell_draw(key, shape, scale, bound, shards=(), kind=jnp.bfloat16):
    result = jax.random.normal(key, shape, jnp.float32) * scale
    if len(shards) > 0:
        result = steps_of(key, shape, shards, -0.22, 0.18) * result
    return jnp.clip(result, min=-bound, max=bound).astype(kind)


def setup_inputs(seed: int = 0, part: int = 0) -> dict:
    keys = jax.random.split(jax.random.key(seed), 8)
    part_splits = jax.random.split(jax.random.fold_in(keys[7], part), 8)
    factor_paths = bell_draw(part_splits[0], (FACTORS, DATES, PATHS), 1.0, 6.0, ((0, 16),))
    loadings = bell_draw(keys[1], (TRADES, REFS * BLOCK_LEN), (REFS * BLOCK_LEN) ** -0.5, 0.75, ((0, 16),))
    coeffs = bell_draw(keys[2], (TRADES, BASIS), 4096 ** -0.5, 0.09375, ((0, 16),))
    trade_blocks_keys = jax.random.split(jax.random.fold_in(keys[3], 1), TRADES // TRADE_DEV)
    trade_blocks_turns = jax.random.permutation(jax.random.fold_in(keys[3], 3), TRADES // TRADE_DEV)
    trade_blocks = jax.vmap(lambda own, number: shared_out(jax.random.fold_in(keys[3], 2), own, number, TRADE_DEV, BLOCKS, REFS, HIT_CAP, 1))(trade_blocks_keys, trade_blocks_turns).reshape((TRADES, REFS))
    trade_set = place_ends(jax.random.randint(keys[4], (TRADES,), 0, NSETS), jax.random.fold_in(keys[4], 1), 0, NSETS - 1).astype(jnp.int32)
    set_order = jax.random.permutation(keys[5], NSETS).astype(jnp.int32)
    owner_counts = ragged_sizes(keys[6], OWNERS, NSETS, SET_CAP, 2).astype(jnp.int32)
    return dict(factor_paths=factor_paths, loadings=loadings, coeffs=coeffs, trade_blocks=trade_blocks, trade_set=trade_set, set_order=set_order, owner_counts=owner_counts)


def chebyshev_sum(under, coef):
    zval = jnp.tanh(under)
    acc = coef[:, 0:1] + coef[:, 1:2] * zval
    before = jnp.ones_like(zval)
    current = zval
    for order in range(2, BASIS):
        after = 2.0 * zval * current - before
        acc = acc + coef[:, order:order + 1] * after
        before = current
        current = after
    return acc


def reference(factor_paths, loadings, coeffs, trade_blocks, trade_set, set_order, owner_counts):
    width = DATES * PATHS
    flat = factor_paths.reshape(FACTORS, width)
    owners = owner_counts.shape[0]
    ends = jnp.cumsum(owner_counts).astype(jnp.int32)
    starts = (ends - owner_counts).astype(jnp.int32)
    rank = set_order[trade_set].astype(jnp.int32)
    owner = jnp.sum((ends[None, :] <= rank[:, None]).astype(jnp.int32), axis=1).astype(jnp.int32)
    row_of = (owner * SET_CAP + rank - starts[owner]).astype(jnp.int32)
    group = TRADE_DEV
    count = loadings.shape[0] // group
    offsets = jnp.arange(BLOCK_LEN, dtype=jnp.int32)

    def step(table, items):
        load, coef, blocks, rows = items
        index = (blocks[:, :, None] * BLOCK_LEN + offsets[None, None, :]).reshape(group, REFS * BLOCK_LEN)
        picked = flat[index].astype(jnp.float32)
        under = jnp.einsum("tj,tjs->ts", load.astype(jnp.float32), picked)
        mtm = chebyshev_sum(under, coef.astype(jnp.float32))
        table = table + jax.ops.segment_sum(mtm, rows, num_segments=owners * SET_CAP)
        return table, None

    items = (loadings.reshape(count, group, -1), coeffs.reshape(count, group, -1),
             trade_blocks.reshape(count, group, -1), row_of.reshape(count, group))
    table, _ = lax.scan(step, jnp.zeros((owners * SET_CAP, width), jnp.float32), items)
    return jnp.maximum(table, 0.0).reshape(owners * SET_CAP, DATES, PATHS)
```

```python
import functools

import jax
import jax.numpy as jnp
import numpy as np
from jax import lax
from jax.experimental import pallas as pl
from jax.experimental.pallas import tpu as pltpu
from jax.sharding import PartitionSpec as P

BLOCK_LEN = 16
REFS = 4
SET_CAP = 32
STEP = 8
MESH = pl.DeviceIdType.MESH


def two_level(basis):
    now = np.eye(basis, dtype=np.float32)
    out = np.zeros((basis, basis), np.float32)
    for a in range(basis // STEP - 1, 0, -1):
        out[a * STEP] = now[a * STEP]
        for b in range(1, STEP):
            out[a * STEP + b] = 2 * now[a * STEP + b]
            now[a * STEP - b] -= now[a * STEP + b]
    out[:STEP] = now[:STEP]
    return out


def kernel(trades, fx, load, coef, blocks, tset, order, counts, mix, out,
           gath, weight, spread, acc, ct, zt, mtm, net, tab, got1, sum1, got2, sum2, got3,
           sz, rz, sy, ry, ss, rs, s1, r1, s2, r2, s3, r3):
    dates, nloc, paths = fx.shape
    local = load.shape[0]
    basis = coef.shape[1]
    half = trades // 2
    owners = trades * 2
    nsets = order.shape[1]
    rows = owners * SET_CAP
    factors = owners * nloc

    t = lax.axis_index("trades")
    c = lax.axis_index("quad")
    hi, lo = t // 2, lax.rem(t, 2)
    sib = {"trades": t, "quad": 1 - c}
    across = {"trades": hi * 2 + (1 - lo), "quad": c}

    def zpos(k):
        return lax.rem(hi + k, half)

    def zdev(k):
        return {"trades": zpos(k) * 2 + lo, "quad": c}

    def shard(h, l, q):
        return (h * 2 + l) * 2 + q

    me = shard(hi, lo, c)

    barrier = pltpu.get_barrier_semaphore()
    for dev in [sib, across] + [zdev(k) for k in range(1, half)]:
        pl.semaphore_signal(barrier, inc=1, device_id=dev, device_id_type=MESH)
    pl.semaphore_wait(barrier, half + 1)

    def rcopy(src, dst, ssem, rsem, dev):
        return pltpu.make_async_remote_copy(
            src_ref=src, dst_ref=dst, send_sem=ssem, recv_sem=rsem,
            device_id=dev, device_id_type=MESH)

    pending = []

    def send(*args):
        cp = rcopy(*args)
        cp.start()
        pending.append(cp)

    def own(d):
        src, dst = fx.at[d], gath.at[d, me]
        for k in range(1, half):
            send(src, dst, sz.at[d, k - 1], rz.at[d, k - 1], zdev(k))
        send(src, dst, sy.at[d, 0], ry.at[d, 0], across)
        send(src, dst, ss.at[d, 0], rs.at[d, 0], sib)

    def arrive_z(d, k):
        slot = gath.at[d, shard(zpos(half - k), lo, c)]
        rcopy(slot, slot, sz.at[d, k - 1], rz.at[d, k - 1], zdev(k)).wait_recv()
        send(slot, slot, sy.at[d, k], ry.at[d, k], across)
        send(slot, slot, ss.at[d, k], rs.at[d, k], sib)

    def arrive_y(d, k):
        slot = gath.at[d, shard(zpos(half - k), 1 - lo, c)]
        rcopy(slot, slot, sy.at[d, k], ry.at[d, k], across).wait_recv()
        send(slot, slot, ss.at[d, half + k], rs.at[d, half + k], sib)

    def arrive_s(d):
        for k in range(half):
            slot = gath.at[d, shard(zpos(half - k), lo, 1 - c)]
            rcopy(slot, slot, ss.at[d, k], rs.at[d, k], sib).wait_recv()
        for k in range(half):
            slot = gath.at[d, shard(zpos(half - k), 1 - lo, 1 - c)]
            rcopy(slot, slot, ss.at[d, half + k], rs.at[d, half + k], sib).wait_recv()

    own(0)
    own(1)

    for d in range(dates):
        gath[d, me] = fx[d]

    ct[...] = lax.dot_general(mix[...], coef[...], (((1,), (1,)), ((), ())),
                              preferred_element_type=jnp.float32)

    j = lax.broadcasted_iota(jnp.int32, (REFS * BLOCK_LEN, 128), 0)
    l = lax.broadcasted_iota(jnp.int32, (REFS * BLOCK_LEN, 128), 1)
    for r in range(REFS):
        pick = jnp.where(j == r * BLOCK_LEN + (l & (BLOCK_LEN - 1)), 1.0, 0.0).astype(jnp.bfloat16)
        spread[r] = jnp.dot(load[...], pick, preferred_element_type=jnp.float32)

    def build(first, count):
        @pl.loop(first, first + count)
        def _(i):
            at = pl.ds(pl.multiple_of(i * 16, 16), 16)
            ids = blocks[at, :]
            lane = lax.broadcasted_iota(jnp.int32, (16, 128), 1) // BLOCK_LEN
            diff = [ids[:, r:r + 1] - lane for r in range(REFS)]
            val = [spread[r, at, :] for r in range(REFS)]
            for n in range(factors // 128):
                v = jnp.zeros((16, 128), jnp.float32)
                for r in range(REFS):
                    v = jnp.where(diff[r] == n * (128 // BLOCK_LEN), val[r], v)
                weight[at, n * 128:(n + 1) * 128] = v.astype(jnp.bfloat16)

    pieces = half
    each = local // 16 // pieces
    for k in range(pieces):
        build(k * each, each)
        if k + 1 < half:
            arrive_z(0, k + 1)

    d0 = lax.broadcasted_iota(jnp.int32, (owners, owners), 0)
    d1 = lax.broadcasted_iota(jnp.int32, (owners, owners), 1)
    cnt = jnp.broadcast_to(counts[...], (owners, owners))
    starts = jnp.sum(jnp.where(d1 < d0, cnt, 0), axis=1, keepdims=True)
    ends = jnp.sum(jnp.where(d1 <= d0, cnt, 0), axis=1, keepdims=True)
    rank = jnp.broadcast_to(order[...], (owners, nsets))
    od = lax.broadcasted_iota(jnp.int32, (owners, nsets), 0)
    place = ((od & 1) * 2 + ((od >> 1) & 1)) * half + (od >> 2)
    mine = (starts <= rank) & (rank < ends)
    where_owner = jnp.sum(jnp.where(mine, place, 0), axis=0, keepdims=True)
    where_slot = jnp.sum(jnp.where(mine, rank - starts, 0), axis=0, keepdims=True)
    sid = lax.broadcasted_iota(jnp.int32, (nsets, local), 0)
    hot = jnp.where(sid == tset[...], 1.0, 0.0).astype(jnp.bfloat16)
    both = jnp.concatenate(
        [jnp.broadcast_to(where_owner, (8, nsets)), jnp.broadcast_to(where_slot, (8, nsets))], axis=0)
    found = jnp.dot(both.astype(jnp.float32).astype(jnp.bfloat16), hot,
                    preferred_element_type=jnp.float32)
    row = (found[0:1, :] * SET_CAP + found[8:9, :]).astype(jnp.int32)
    rid = lax.broadcasted_iota(jnp.int32, (rows, local), 0)
    net[...] = jnp.where(rid == row, 1.0, 0.0).astype(jnp.bfloat16)

    for k in range(half):
        arrive_y(0, k)
    arrive_s(0)

    per = 2048 // nloc

    def multiply(d):
        acc[...] = jnp.zeros_like(acc)

        @pl.loop(0, owners // per)
        def _(i):
            cols = pl.ds(pl.multiple_of(i * (per * nloc), 128), per * nloc)
            part = gath[d, pl.ds(i * per, per)].reshape(per * nloc, paths)
            acc[...] += jnp.dot(weight[:, cols], part, preferred_element_type=jnp.float32)

    def price():
        @pl.loop(0, local // 128)
        def _(i):
            at = pl.ds(pl.multiple_of(i * 128, 128), 128)
            zt[...] = jnp.tanh(acc[at, :].T)
            for p in range(paths // 32):
                z = zt[p * 32:(p + 1) * 32, :]
                z2 = z + z
                tk = [None, z]
                for b in range(2, STEP + 1):
                    tk.append(z2 * tk[b - 1] - (1.0 if b == 2 else tk[b - 2]))
                y = tk[STEP]
                y2 = y + y
                b1 = b2 = None
                for a in range(basis // STEP - 1, -1, -1):
                    q = jnp.broadcast_to(ct[a * STEP:a * STEP + 1, at], z.shape)
                    for b in range(1, STEP):
                        q = q + ct[a * STEP + b:a * STEP + b + 1, at] * tk[b]
                    if b1 is None:
                        new = q
                    elif b2 is None:
                        new = q + (y if a == 0 else y2) * b1
                    else:
                        new = q + ((y if a == 0 else y2) * b1 - b2)
                    b1, b2 = new, b1
                high = b1.astype(jnp.bfloat16)
                mtm[p * 32:(p + 1) * 32, at] = high
                mtm[paths + p * 32:paths + (p + 1) * 32, at] = (
                    b1 - high.astype(jnp.float32)).astype(jnp.bfloat16)

    h1, h2 = rows // 2, rows // 4

    def netting(d):
        full = lax.dot_general(net[...], mtm[...], (((1,), (1,)), ((), ())),
                               preferred_element_type=jnp.float32)
        tab[d] = full[:, :paths] + full[:, paths:]
        away = pl.multiple_of((1 - c) * h1, h1)
        send(tab.at[d, pl.ds(away, h1)], got1.at[d], s1.at[d], r1.at[d], sib)

    def stage2(d):
        rcopy(got1.at[d], got1.at[d], s1.at[d], r1.at[d], sib).wait_recv()
        sum1[d] = tab[d, pl.ds(pl.multiple_of(c * h1, h1), h1)] + got1[d]
        away = pl.multiple_of((1 - lo) * h2, h2)
        send(sum1.at[d, pl.ds(away, h2)], got2.at[d], s2.at[d], r2.at[d], across)

    def stage3(d):
        rcopy(got2.at[d], got2.at[d], s2.at[d], r2.at[d], across).wait_recv()
        sum2[d] = sum1[d, pl.ds(pl.multiple_of(lo * h2, h2), h2)] + got2[d]
        for k in range(1, half):
            src = sum2.at[d, pl.ds(pl.multiple_of(zpos(k) * SET_CAP, SET_CAP), SET_CAP)]
            send(src, got3.at[d, k - 1], s3.at[d, k - 1], r3.at[d, k - 1], zdev(k))

    def finish(d):
        total = sum2[d, pl.ds(pl.multiple_of(hi * SET_CAP, SET_CAP), SET_CAP)]
        for k in range(1, half):
            slot = got3.at[d, k - 1]
            rcopy(slot, slot, s3.at[d, k - 1], r3.at[d, k - 1], zdev(k)).wait_recv()
            total = total + got3[d, k - 1]
        out[d] = jnp.maximum(total, 0.0)

    for d in range(dates):
        if d + 2 < dates:
            own(d + 2)
        multiply(d)
        if d + 1 < dates:
            for k in range(1, half):
                arrive_z(d + 1, k)
        price()
        netting(d)
        if d + 1 < dates:
            for k in range(half):
                arrive_y(d + 1, k)
        stage2(d)
        stage3(d)
        if d + 1 < dates:
            arrive_s(d + 1)
    for d in range(dates):
        finish(d)
    for cp in pending:
        cp.wait_send()


def on_device(trades, factor_paths, loadings, coeffs, trade_blocks, trade_set, set_order, owner_counts):
    nloc, dates, paths = factor_paths.shape
    local = loadings.shape[0]
    basis = coeffs.shape[1]
    owners = 2 * trades
    half = trades // 2
    rows = owners * SET_CAP
    dma = pltpu.SemaphoreType.DMA
    fx = jnp.transpose(factor_paths, (1, 0, 2))
    f32, bf16 = jnp.float32, jnp.bfloat16
    result = pl.pallas_call(
        functools.partial(kernel, trades),
        out_shape=jax.ShapeDtypeStruct((dates, SET_CAP, paths), f32),
        in_specs=[pl.BlockSpec(memory_space=pltpu.VMEM)] * 8,
        out_specs=pl.BlockSpec(memory_space=pltpu.VMEM),
        scratch_shapes=[
            pltpu.VMEM((dates, owners, nloc, paths), bf16),
            pltpu.VMEM((local, owners * nloc), bf16),
            pltpu.VMEM((REFS, local, 128), f32),
            pltpu.VMEM((local, paths), f32),
            pltpu.VMEM((basis, local), f32),
            pltpu.VMEM((paths, 128), f32),
            pltpu.VMEM((2 * paths, local), bf16),
            pltpu.VMEM((rows, local), bf16),
            pltpu.VMEM((dates, rows, paths), f32),
            pltpu.VMEM((dates, rows // 2, paths), f32),
            pltpu.VMEM((dates, rows // 2, paths), f32),
            pltpu.VMEM((dates, rows // 4, paths), f32),
            pltpu.VMEM((dates, rows // 4, paths), f32),
            pltpu.VMEM((dates, half - 1, SET_CAP, paths), f32),
            dma((dates, half - 1)), dma((dates, half - 1)),
            dma((dates, half)), dma((dates, half)),
            dma((dates, 2 * half)), dma((dates, 2 * half)),
            dma((dates,)), dma((dates,)),
            dma((dates,)), dma((dates,)),
            dma((dates, half - 1)), dma((dates, half - 1)),
        ],
        compiler_params=pltpu.CompilerParams(
            collective_id=0, has_side_effects=True, vmem_limit_bytes=56 * 1024 * 1024
        ),
    )(
        fx, loadings, coeffs, trade_blocks, trade_set.reshape(1, -1),
        set_order.reshape(1, -1), owner_counts.reshape(1, -1),
        jnp.asarray(two_level(basis), bf16),
    )
    return jnp.transpose(result, (1, 0, 2))


def solution(mesh):
    in_specs = (
        P(("trades", "quad"), None, "paths"),
        P(("trades", "quad"), None),
        P(("trades", "quad"), None),
        P(("trades", "quad"), None),
        P(("trades", "quad")),
        P(),
        P(),
    )
    out_specs = P(("trades", "quad"), None, "paths")
    return jax.shard_map(
        functools.partial(on_device, mesh.shape["trades"]),
        mesh=mesh, in_specs=in_specs, out_specs=out_specs, check_vma=False,
    )
```

```python
import functools

import jax
import jax.numpy as jnp
import numpy as np
from jax import lax
from jax.experimental import pallas as pl
from jax.experimental.pallas import tpu as pltpu
from jax.sharding import PartitionSpec as P

BLOCK_LEN = 16
REFS = 4
SET_CAP = 32
STEP = 8
MESH = pl.DeviceIdType.MESH


def two_level(basis):
    now = np.eye(basis, dtype=np.float32)
    out = np.zeros((basis, basis), np.float32)
    for a in range(basis // STEP - 1, 0, -1):
        out[a * STEP] = now[a * STEP]
        for b in range(1, STEP):
            out[a * STEP + b] = 2 * now[a * STEP + b]
            now[a * STEP - b] -= now[a * STEP + b]
    out[:STEP] = now[:STEP]
    return out


def kernel(trades, fx, load, coef, blocks, tset, order, counts, mix, out,
           gath, weight, spread, acc, ct, zt, mtm, net, tab, got1, sum1, got2, sum2, got3,
           sz, rz, sy, ry, ss, rs, s1, r1, s2, r2, s3, r3):
    dates, nloc, paths = fx.shape
    local = load.shape[0]
    basis = coef.shape[1]
    half = trades // 2
    owners = trades * 2
    nsets = order.shape[1]
    rows = owners * SET_CAP
    factors = owners * nloc

    t = lax.axis_index("trades")
    c = lax.axis_index("quad")
    hi, lo = t // 2, lax.rem(t, 2)
    sib = {"trades": t, "quad": 1 - c}
    across = {"trades": hi * 2 + (1 - lo), "quad": c}

    def zpos(k):
        return lax.rem(hi + k, half)

    def zdev(k):
        return {"trades": zpos(k) * 2 + lo, "quad": c}

    def shard(h, l, q):
        return (h * 2 + l) * 2 + q

    me = shard(hi, lo, c)

    barrier = pltpu.get_barrier_semaphore()
    for dev in [sib, across] + [zdev(k) for k in range(1, half)]:
        pl.semaphore_signal(barrier, inc=1, device_id=dev, device_id_type=MESH)
    pl.semaphore_wait(barrier, half + 1)

    def rcopy(src, dst, ssem, rsem, dev):
        return pltpu.make_async_remote_copy(
            src_ref=src, dst_ref=dst, send_sem=ssem, recv_sem=rsem,
            device_id=dev, device_id_type=MESH)

    pending = []

    def send(*args):
        cp = rcopy(*args)
        cp.start()
        pending.append(cp)

    relayed = half == 4
    edge = (hi == 0) | (hi == half - 1)

    ks = list(range(1, half, 2)) + list(range(2, half, 2))

    def part_of(d, s):
        return gath.at[d // 2, s, d % 2]

    def own_near(d):
        send(fx.at[d], part_of(d, me), sy.at[d, 0], ry.at[d, 0], across)
        send(fx.at[d], part_of(d, me), ss.at[d, 0], rs.at[d, 0], sib)

    def own_far(d):
        for k in ks:
            cp = rcopy(fx.at[d], part_of(d, me), sz.at[d, k - 1], rz.at[d, k - 1], zdev(k))
            if relayed and k == 2:
                pl.when(edge)(cp.start)
            else:
                cp.start()
            pending.append(cp)

    def arrive_z(d, k):
        slot = part_of(d, shard(zpos(half - k), lo, c))
        rcopy(slot, slot, sz.at[d, k - 1], rz.at[d, k - 1], zdev(k)).wait_recv()
        if relayed and k != 2:
            passer, step = (2, 1) if k == 1 else (1, 3)
            relay = rcopy(slot, slot, sz.at[d, 1], rz.at[d, 1], zdev(step))
            pl.when(hi == passer)(relay.start)
        send(slot, slot, sy.at[d, k], ry.at[d, k], across)
        send(slot, slot, ss.at[d, k], rs.at[d, k], sib)

    def arrive_y(d, k):
        slot = part_of(d, shard(zpos(half - k), 1 - lo, c))
        rcopy(slot, slot, sy.at[d, k], ry.at[d, k], across).wait_recv()
        send(slot, slot, ss.at[d, half + k], rs.at[d, half + k], sib)

    def multiply(e, k, side):
        l = lo if side == 0 else 1 - lo
        n = side * half + k
        h = zpos(half - k)
        for d in (2 * e, 2 * e + 1):
            slot = part_of(d, shard(h, l, 1 - c))
            rcopy(slot, slot, ss.at[d, n], rs.at[d, n], sib).wait_recv()
        first = shard(h, l, 0)
        cols = pl.ds(pl.multiple_of(first * nloc, 2 * nloc), 2 * nloc)
        part = jnp.concatenate(
            [jnp.concatenate([gath[e, first + q, 0], gath[e, first + q, 1]], axis=1)
             for q in range(2)], axis=0)
        new = jnp.dot(weight[:, cols], part, preferred_element_type=jnp.float32)
        if n == 0:
            acc[e] = new
        else:
            acc[e] += new

    own_far(0)
    for d in range(dates):
        own_near(d)
    own_far(1)

    for d in range(dates):
        gath[d // 2, me, d % 2] = fx[d]

    ct[...] = lax.dot_general(mix[...], coef[...], (((1,), (1,)), ((), ())),
                              preferred_element_type=jnp.float32)

    j = lax.broadcasted_iota(jnp.int32, (REFS * BLOCK_LEN, 128), 0)
    l = lax.broadcasted_iota(jnp.int32, (REFS * BLOCK_LEN, 128), 1)
    for r in range(REFS):
        pick = jnp.where(j == r * BLOCK_LEN + (l & (BLOCK_LEN - 1)), 1.0, 0.0).astype(jnp.bfloat16)
        spread[r] = jnp.dot(load[...], pick, preferred_element_type=jnp.float32)

    def build(first, count):
        @pl.loop(first, first + count)
        def _(i):
            at = pl.ds(pl.multiple_of(i * 16, 16), 16)
            ids = blocks[at, :]
            lane = lax.broadcasted_iota(jnp.int32, (16, 128), 1) // BLOCK_LEN
            diff = [ids[:, r:r + 1] - lane for r in range(REFS)]
            val = [spread[r, at, :] for r in range(REFS)]
            for n in range(factors // 128):
                v = jnp.zeros((16, 128), jnp.float32)
                for r in range(REFS):
                    v = jnp.where(diff[r] == n * (128 // BLOCK_LEN), val[r], v)
                weight[at, n * 128:(n + 1) * 128] = v.astype(jnp.bfloat16)

    each = local // 16 // (2 * half)
    for n in range(2 * half):
        build(n * each, each)
        d, k = divmod(n, half)
        if k > 0:
            arrive_z(d, ks[k - 1])
            if k + 1 == half:
                own_far(d + 2)

    d0 = lax.broadcasted_iota(jnp.int32, (owners, owners), 0)
    d1 = lax.broadcasted_iota(jnp.int32, (owners, owners), 1)
    cnt = jnp.broadcast_to(counts[...], (owners, owners))
    starts = jnp.sum(jnp.where(d1 < d0, cnt, 0), axis=1, keepdims=True)
    ends = jnp.sum(jnp.where(d1 <= d0, cnt, 0), axis=1, keepdims=True)
    rank = jnp.broadcast_to(order[...], (owners, nsets))
    od = lax.broadcasted_iota(jnp.int32, (owners, nsets), 0)
    place = ((od & 1) * 2 + ((od >> 1) & 1)) * half + (od >> 2)
    mine = (starts <= rank) & (rank < ends)
    where_owner = jnp.sum(jnp.where(mine, place, 0), axis=0, keepdims=True)
    where_slot = jnp.sum(jnp.where(mine, rank - starts, 0), axis=0, keepdims=True)
    sid = lax.broadcasted_iota(jnp.int32, (nsets, local), 0)
    hot = jnp.where(sid == tset[...], 1.0, 0.0).astype(jnp.bfloat16)
    both = jnp.concatenate(
        [jnp.broadcast_to(where_owner, (8, nsets)), jnp.broadcast_to(where_slot, (8, nsets))], axis=0)
    found = jnp.dot(both.astype(jnp.float32).astype(jnp.bfloat16), hot,
                    preferred_element_type=jnp.float32)
    row = (found[0:1, :] * SET_CAP + found[8:9, :]).astype(jnp.int32)
    rid = lax.broadcasted_iota(jnp.int32, (rows, local), 0)
    net[...] = jnp.where(rid == row, 1.0, 0.0).astype(jnp.bfloat16)

    def price(d):
        @pl.loop(0, local // 128)
        def _(i):
            at = pl.ds(pl.multiple_of(i * 128, 128), 128)
            zt[...] = jnp.tanh(acc[d // 2, at, (d % 2) * paths:(d % 2 + 1) * paths].T)
            for p in range(paths // 32):
                z = zt[p * 32:(p + 1) * 32, :]
                z2 = z + z
                tk = [None, z]
                for b in range(2, STEP + 1):
                    tk.append(z2 * tk[b - 1] - (1.0 if b == 2 else tk[b - 2]))
                y = tk[STEP]
                y2 = y + y
                b1 = b2 = None
                for a in range(basis // STEP - 1, -1, -1):
                    q = jnp.broadcast_to(ct[a * STEP:a * STEP + 1, at], z.shape)
                    for b in range(1, STEP):
                        q = q + ct[a * STEP + b:a * STEP + b + 1, at] * tk[b]
                    if b1 is None:
                        new = q
                    elif b2 is None:
                        new = q + (y if a == 0 else y2) * b1
                    else:
                        new = q + ((y if a == 0 else y2) * b1 - b2)
                    b1, b2 = new, b1
                high = b1.astype(jnp.bfloat16)
                mtm[p * 32:(p + 1) * 32, at] = high
                mtm[paths + p * 32:paths + (p + 1) * 32, at] = (
                    b1 - high.astype(jnp.float32)).astype(jnp.bfloat16)

    h1, h2 = rows // 2, rows // 4

    def netting(d):
        full = lax.dot_general(net[...], mtm[...], (((1,), (1,)), ((), ())),
                               preferred_element_type=jnp.float32)
        tab[d] = full[:, :paths] + full[:, paths:]
        away = pl.multiple_of((1 - c) * h1, h1)
        send(tab.at[d, pl.ds(away, h1)], got1.at[d], s1.at[d], r1.at[d], sib)

    def stage2(d):
        rcopy(got1.at[d], got1.at[d], s1.at[d], r1.at[d], sib).wait_recv()
        sum1[d] = tab[d, pl.ds(pl.multiple_of(c * h1, h1), h1)] + got1[d]
        away = pl.multiple_of((1 - lo) * h2, h2)
        send(sum1.at[d, pl.ds(away, h2)], got2.at[d], s2.at[d], r2.at[d], across)

    def stage3(d):
        rcopy(got2.at[d], got2.at[d], s2.at[d], r2.at[d], across).wait_recv()
        sum2[d] = sum1[d, pl.ds(pl.multiple_of(lo * h2, h2), h2)] + got2[d]
        for k in range(1, half):
            src = sum2.at[d, pl.ds(pl.multiple_of(zpos(k) * SET_CAP, SET_CAP), SET_CAP)]
            send(src, got3.at[d, k - 1], s3.at[d, k - 1], r3.at[d, k - 1], zdev(k))

    def finish(d):
        total = sum2[d, pl.ds(pl.multiple_of(hi * SET_CAP, SET_CAP), SET_CAP)]
        for k in range(1, half):
            slot = got3.at[d, k - 1]
            rcopy(slot, slot, s3.at[d, k - 1], r3.at[d, k - 1], zdev(k)).wait_recv()
            total = total + got3[d, k - 1]
        out[d] = jnp.maximum(total, 0.0)

    def cross(e, k):
        arrive_y(2 * e, k)
        arrive_y(2 * e + 1, k)

    multiply(0, 0, 0)
    cross(0, 0)
    for n, k in enumerate(ks):
        multiply(0, k, 0)
        cross(0, k)
        arrive_z(2, k)
        multiply(0, ([0] + ks)[n], 1)
    for k in ks:
        arrive_z(3, k)
    multiply(0, ks[-1], 1)
    price(0)
    netting(0)
    multiply(1, 0, 0)
    cross(1, 0)
    stage2(0)
    multiply(1, ks[0], 0)
    stage3(0)
    multiply(1, 0, 1)
    cross(1, ks[0])
    price(1)
    netting(1)
    for n in range(1, len(ks)):
        multiply(1, ks[n], 0)
        multiply(1, ks[n - 1], 1)
        cross(1, ks[n])
        if n == 1:
            stage2(1)
        if n == 2:
            stage3(1)
    multiply(1, ks[-1], 1)
    price(2)
    netting(2)
    stage2(2)
    price(3)
    stage3(2)
    netting(3)
    stage2(3)
    stage3(3)
    for d in range(dates):
        finish(d)
    for cp in pending:
        cp.wait_send()


def on_device(trades, factor_paths, loadings, coeffs, trade_blocks, trade_set, set_order, owner_counts):
    nloc, dates, paths = factor_paths.shape
    local = loadings.shape[0]
    basis = coeffs.shape[1]
    owners = 2 * trades
    half = trades // 2
    rows = owners * SET_CAP
    dma = pltpu.SemaphoreType.DMA
    fx = jnp.transpose(factor_paths, (1, 0, 2))
    f32, bf16 = jnp.float32, jnp.bfloat16
    result = pl.pallas_call(
        functools.partial(kernel, trades),
        out_shape=jax.ShapeDtypeStruct((dates, SET_CAP, paths), f32),
        in_specs=[pl.BlockSpec(memory_space=pltpu.VMEM)] * 8,
        out_specs=pl.BlockSpec(memory_space=pltpu.VMEM),
        scratch_shapes=[
            pltpu.VMEM((dates // 2, owners, 2, nloc, paths), bf16),
            pltpu.VMEM((local, owners * nloc), bf16),
            pltpu.VMEM((REFS, local, 128), f32),
            pltpu.VMEM((dates // 2, local, 2 * paths), f32),
            pltpu.VMEM((basis, local), f32),
            pltpu.VMEM((paths, 128), f32),
            pltpu.VMEM((2 * paths, local), bf16),
            pltpu.VMEM((rows, local), bf16),
            pltpu.VMEM((dates, rows, paths), f32),
            pltpu.VMEM((dates, rows // 2, paths), f32),
            pltpu.VMEM((dates, rows // 2, paths), f32),
            pltpu.VMEM((dates, rows // 4, paths), f32),
            pltpu.VMEM((dates, rows // 4, paths), f32),
            pltpu.VMEM((dates, half - 1, SET_CAP, paths), f32),
            dma((dates, half - 1)), dma((dates, half - 1)),
            dma((dates, half)), dma((dates, half)),
            dma((dates, 2 * half)), dma((dates, 2 * half)),
            dma((dates,)), dma((dates,)),
            dma((dates,)), dma((dates,)),
            dma((dates, half - 1)), dma((dates, half - 1)),
        ],
        compiler_params=pltpu.CompilerParams(
            collective_id=0, has_side_effects=True, vmem_limit_bytes=56 * 1024 * 1024
        ),
    )(
        fx, loadings, coeffs, trade_blocks, trade_set.reshape(1, -1),
        set_order.reshape(1, -1), owner_counts.reshape(1, -1),
        jnp.asarray(two_level(basis), bf16),
    )
    return jnp.transpose(result, (1, 0, 2))


def solution(mesh):
    in_specs = (
        P(("trades", "quad"), None, "paths"),
        P(("trades", "quad"), None),
        P(("trades", "quad"), None),
        P(("trades", "quad"), None),
        P(("trades", "quad")),
        P(),
        P(),
    )
    out_specs = P(("trades", "quad"), None, "paths")
    return jax.shard_map(
        functools.partial(on_device, mesh.shape["trades"]),
        mesh=mesh, in_specs=in_specs, out_specs=out_specs, check_vma=False,
    )
```
